32 devices in a mesh: sec: 4 (over z), row: 2 (over x), inner: 4 (over y, core).
Axes of the slice: x: 2, y: 2, z: 4, core: 2. Of those that a mesh axis runs over, the one named last changes fastest.
Arguments:
- amplitudes: bfloat16 [256, 4, 16384], P('row', 'inner'), may hold values from -6 to 6
- hole_ladder: bfloat16 [256, 256], P('row'), may hold values from -0.375 to 0.375
- bare_integrals: bfloat16 [256, 4, 16384], P('row', 'inner', 'sec'), may hold values from -6 to 6
- ladder_tiles: bfloat16 [1024, 512, 128], P('sec', 'inner'), may hold values from -0.1875 to 0.1875
- ladder_source: int32 [1024, 4], P('sec', 'inner'), may hold values from 0 to 127
- ladder_target: int32 [1024, 4], P('sec', 'inner'), may hold values from 0 to 127
- ladder_live: int32 [4, 4], P('sec', 'inner'), may hold values from 64 to 256, as said below
- cycle_tiles: bfloat16 [128, 512, 128], P('sec', 'inner'), may hold values from -0.5 to 0.5
- cycle_source: int32 [128, 4], P('sec', 'inner'), may hold values from 0 to 63
- cycle_target: int32 [128, 4], P('sec', 'inner'), may hold values from 0 to 127
- gap_rows: int32 [256], P('row'), may hold values from 512 to 2047
- gap_columns: int32 [4, 16384], P('inner', 'sec'), may hold values from 512 to 2047
Outputs:
- updated: bfloat16 [256, 4, 16384], P('row', 'inner', 'sec')
The draws below stay inside these ranges and needn't reach their ends.
Inputs may be any that keep to these rules, and one draw needn't show every extreme that they name: Slots from ladder_live on are padding and carry no term; some section and quarter has all 256 slots live in every draw.
All inputs are finite; a program needn't handle non-finite values.
Results may differ from the reference program's by a relative error of at most 0.0095.
Values may be sent and summed in bfloat16 or wider, within the bound.
A program may use at most 128 MiB of HBM per device.

```python
import jax
import jax.numpy as jnp

V_PAIRS = 65536
TILE = 128
PANEL = 2048
TILE_DEV = 256
CYCLE_DEV = 32
ROWS = 256
QUARTER = 16384
QUARTER_BLOCKS = 128
PANEL_BLOCKS = 64
N_SEC = 4
N_INNER = 4


def draw_ladder_live(key, part):
    first_key, second_key = jax.random.split(jax.random.fold_in(key, 17))
    counts = jax.random.randint(first_key, (N_SEC * N_INNER,), TILE_DEV // 4, TILE_DEV + 1)
    chosen = jax.random.randint(second_key, (), 0, N_SEC * N_INNER)
    counts = jnp.where(jnp.arange(N_SEC * N_INNER) == chosen, TILE_DEV, counts)
    return counts.reshape(N_SEC, N_INNER).astype(jnp.int32)


def set_ends(values, own_key, least, high):
    dims = values.shape
    index_at = [jax.random.randint(jax.random.fold_in(own_key, axis), (), 0, dims[axis]) for axis in range(len(dims))]
    values = values.at[tuple(index_at)].set(least)
    longest = dims.index(max(dims))
    index_at[longest] = (index_at[longest] + 1) % dims[longest]
    return values.at[tuple(index_at)].set(high)


def level_of(own_key, extent, pieces, smallest, top_value):
    level = 1.0
    for axis_at, parts in pieces:
        heights = jax.random.uniform(jax.random.fold_in(jax.random.fold_in(own_key, 6), axis_at), (parts,), jnp.float32, smallest / len(pieces), top_value / len(pieces))
        level = level * jnp.repeat(jnp.exp(heights), extent[axis_at] // parts).reshape((-1,) + (1,) * (len(extent) - 1 - axis_at))
    return level


def gaussian(own_key, dims, scale, bound, cuts=(), held_as=jnp.bfloat16):
    drawn = jax.random.normal(own_key, dims, jnp.float32) * scale
    if len(cuts) > 0:
        drawn = level_of(own_key, dims, cuts, -0.22, 0.18) * drawn
    return jnp.clip(drawn, min=-bound, max=bound).astype(held_as)


def setup_inputs(seed: int = 0) -> dict:
    key_list = jax.random.split(jax.random.key(seed), 13)
    return {
        "amplitudes": gaussian(key_list[0], (ROWS, N_INNER, QUARTER), 1.0, 6.0, ((0, 2), (1, 4))),
        "hole_ladder": gaussian(key_list[1], (ROWS, ROWS), ROWS ** -0.5, 0.375, ((0, 2),)),
        "bare_integrals": gaussian(key_list[2], (ROWS, N_INNER, QUARTER), 1.0, 6.0, ((0, 2), (1, 4), (2, 4))),
        "ladder_tiles": gaussian(key_list[3], (N_SEC * TILE_DEV, N_INNER * TILE, TILE), (TILE * max(1, N_SEC * TILE_DEV // QUARTER_BLOCKS)) ** -0.5, 0.1875, ((0, 4), (1, 4))),
        "ladder_source": set_ends(jax.random.randint(key_list[4], (N_SEC * TILE_DEV, N_INNER), 0, QUARTER_BLOCKS), jax.random.fold_in(key_list[4], 1), 0, QUARTER_BLOCKS - 1).astype(jnp.int32),
        "ladder_target": set_ends(jax.random.randint(key_list[5], (N_SEC * TILE_DEV, N_INNER), 0, QUARTER_BLOCKS), jax.random.fold_in(key_list[5], 1), 0, QUARTER_BLOCKS - 1).astype(jnp.int32),
        "ladder_live": draw_ladder_live(jax.random.fold_in(key_list[12], 71), 0),
        "cycle_tiles": gaussian(key_list[7], (N_SEC * CYCLE_DEV, N_INNER * TILE, TILE), (TILE * max(1, N_SEC * CYCLE_DEV // QUARTER_BLOCKS)) ** -0.5, 0.5, ((0, 4), (1, 4))),
        "cycle_source": set_ends(jax.random.randint(key_list[8], (N_SEC * CYCLE_DEV, N_INNER), 0, PANEL_BLOCKS), jax.random.fold_in(key_list[8], 1), 0, PANEL_BLOCKS - 1).astype(jnp.int32),
        "cycle_target": set_ends(jax.random.randint(key_list[9], (N_SEC * CYCLE_DEV, N_INNER), 0, QUARTER_BLOCKS), jax.random.fold_in(key_list[9], 1), 0, QUARTER_BLOCKS - 1).astype(jnp.int32),
        "gap_rows": set_ends(jax.random.randint(key_list[10], (ROWS,), 512, 2048), jax.random.fold_in(key_list[10], 1), 512, 2047).astype(jnp.int32),
        "gap_columns": set_ends(jax.random.randint(key_list[11], (N_INNER, QUARTER), 512, 2048), jax.random.fold_in(key_list[11], 1), 512, 2047).astype(jnp.int32),
    }


def tile_term(source_blocks, tiles, sources, targets, live_count, block_count):
    tile_count = tiles.shape[0]
    picked = jnp.take(source_blocks, sources, axis=1)
    contribution = jnp.einsum("rtk,tkc->rtc", picked.astype(jnp.float32), tiles.astype(jnp.float32))
    keep_mask = (jnp.arange(tile_count) < live_count).astype(jnp.float32)
    contribution = contribution * keep_mask[None, :, None]
    totals = jnp.zeros((source_blocks.shape[0], block_count, TILE), jnp.float32)
    return totals.at[:, targets].add(contribution)


def reference(amplitudes, hole_ladder, bare_integrals, ladder_tiles, ladder_source, ladder_target, ladder_live, cycle_tiles, cycle_source, cycle_target, gap_rows, gap_columns):
    quarter_width = V_PAIRS // N_INNER
    block_count = quarter_width // TILE
    panel = amplitudes[:, :, :PANEL].reshape(ROWS, N_INNER * PANEL // TILE, TILE)
    quarters = []
    for quarter in range(N_INNER):
        own_blocks = amplitudes[:, quarter, :].reshape(ROWS, block_count, TILE)
        residual = bare_integrals[:, quarter, :].astype(jnp.float32)
        residual = residual + jnp.dot(hole_ladder, amplitudes[:, quarter, :], preferred_element_type=jnp.float32)
        for section in range(N_SEC):
            ladder_slots = slice(section * TILE_DEV, (section + 1) * TILE_DEV)
            cycle_slots = slice(section * CYCLE_DEV, (section + 1) * CYCLE_DEV)
            tile_rows = slice(quarter * TILE, (quarter + 1) * TILE)
            ladder_part = tile_term(own_blocks, ladder_tiles[ladder_slots, tile_rows, :], ladder_source[ladder_slots, quarter], ladder_target[ladder_slots, quarter], ladder_live[section, quarter], block_count)
            cycle_part = tile_term(panel, cycle_tiles[cycle_slots, tile_rows, :], cycle_source[cycle_slots, quarter], cycle_target[cycle_slots, quarter], CYCLE_DEV, block_count)
            share = (ladder_part + cycle_part).reshape(ROWS, quarter_width).astype(jnp.bfloat16)
            residual = residual + share.astype(jnp.float32)
        denominator = (gap_rows[:, None] + gap_columns[quarter][None, :]).astype(jnp.float32) / 1024.0
        quarters.append((residual / denominator).astype(jnp.bfloat16))
    return jnp.stack(quarters, axis=1)
```

```python
import functools

import jax
import jax.numpy as jnp
from jax import lax
from jax.experimental import pallas as pl
from jax.experimental.pallas import tpu as pltpu
from jax.sharding import PartitionSpec as P

TILE = 128
PANEL = 2048
GROUP = 32
UNROLL = 8
PIECES = 2
VMEM = 48 * 1024 * 1024


def ladder_kernel(sources, targets, live, amps, tiles, out, acc):
    step = pl.program_id(0)
    blocks_per_chunk = out.shape[2] // TILE

    @pl.when(step == 0)
    def _():
        @pl.loop(0, acc.shape[0])
        def _(b):
            acc[b] = jnp.zeros(acc.shape[1:], jnp.float32)

    here = jnp.clip(live[0] - step * tiles.shape[0], 0, tiles.shape[0])

    def product(t):
        s = pl.multiple_of(sources[step * tiles.shape[0] + t] * TILE, TILE)
        return jnp.dot(amps[:, pl.ds(s, TILE)], tiles[t], preferred_element_type=jnp.float32)

    def add(t, value):
        b = targets[step * tiles.shape[0] + t]
        acc[b] = acc[b] + value

    full = here // UNROLL

    @pl.loop(0, full)
    def _(g):
        values = [product(g * UNROLL + u) for u in range(UNROLL)]
        for u in range(UNROLL):
            add(g * UNROLL + u, values[u])

    @pl.loop(full * UNROLL, here)
    def _(t):
        add(t, product(t))

    @pl.when(step == pl.num_programs(0) - 1)
    def _():
        for c in range(out.shape[0]):

            @pl.loop(0, blocks_per_chunk)
            def _(b):
                columns = pl.ds(pl.multiple_of(b * TILE, TILE), TILE)
                out[c, :, columns] = acc[c * blocks_per_chunk + b].astype(out.dtype)


def ladder_term(amps, tiles, sources, targets, live, chunk_count):
    rows, width = amps.shape
    count = tiles.shape[0]
    group = GROUP if count % GROUP == 0 else count
    chunk = width // chunk_count
    return pl.pallas_call(
        ladder_kernel,
        grid_spec=pltpu.PrefetchScalarGridSpec(
            num_scalar_prefetch=3,
            grid=(count // group,),
            in_specs=[
                pl.BlockSpec((rows, width), lambda g, s, t, n: (0, 0)),
                pl.BlockSpec(
                    (group, TILE, TILE),
                    lambda g, s, t, n: (jnp.minimum(g, jnp.maximum(n[0] - 1, 0) // group), 0, 0),
                ),
            ],
            out_specs=pl.BlockSpec((chunk_count, rows, chunk), lambda g, s, t, n: (0, 0, 0)),
            scratch_shapes=[pltpu.VMEM((width // TILE, rows, TILE), jnp.float32)],
        ),
        out_shape=jax.ShapeDtypeStruct((chunk_count, rows, chunk), jnp.bfloat16),
        compiler_params=pltpu.CompilerParams(vmem_limit_bytes=VMEM),
        cost_estimate=pl.CostEstimate(
            flops=8 * count * rows * TILE * TILE, bytes_accessed=40 * 1024 * 1024, transcendentals=0
        ),
        name="ladder",
    )(sources, targets, live, amps, tiles)


def cycle_kernel(slots, blocks, targets, chunks, ladder, tiles, *rest):
    pieces, out, panel, acc, sems = rest[:-4], rest[-4], rest[-3], rest[-2], rest[-1]
    step = pl.program_id(0)
    blocks_per_chunk = acc.shape[0]
    first = chunks[step] * blocks_per_chunk
    copies = [pltpu.make_async_copy(p, panel.at[j], sems.at[j]) for j, p in enumerate(pieces)]

    @pl.when(step == 0)
    def _():
        for copy in copies:
            copy.start()

    @pl.loop(0, blocks_per_chunk)
    def _(b):
        columns = pl.ds(pl.multiple_of(b * TILE, TILE), TILE)
        acc[b] = ladder[0, :, columns].astype(jnp.float32)

    @pl.when(step == 0)
    def _():
        for copy in copies:
            copy.wait()

    @pl.loop(0, tiles.shape[0])
    def _(t):
        b = targets[t] - first

        @pl.when((b >= 0) & (b < blocks_per_chunk))
        def _():
            columns = pl.ds(pl.multiple_of(blocks[t] * TILE, TILE), TILE)
            acc[b] = acc[b] + jnp.dot(
                panel[slots[t], :, columns], tiles[t], preferred_element_type=jnp.float32
            )

    @pl.loop(0, blocks_per_chunk)
    def _(b):
        columns = pl.ds(pl.multiple_of(b * TILE, TILE), TILE)
        out[0, :, columns] = acc[b].astype(out.dtype)


def add_cycle(ladder, tiles, pieces, slots, blocks, targets, chunks):
    _, rows, chunk = ladder.shape
    count = chunks.shape[0]
    return pl.pallas_call(
        cycle_kernel,
        grid_spec=pltpu.PrefetchScalarGridSpec(
            num_scalar_prefetch=4,
            grid=(count,),
            in_specs=[
                pl.BlockSpec((1, rows, chunk), lambda i, s, b, t, c: (c[i], 0, 0)),
                pl.BlockSpec(tiles.shape, lambda i, s, b, t, c: (0, 0, 0)),
            ]
            + [pl.BlockSpec(memory_space=pl.ANY)] * len(pieces),
            out_specs=pl.BlockSpec((1, rows, chunk), lambda i, s, b, t, c: (i, 0, 0)),
            scratch_shapes=[
                pltpu.VMEM((len(pieces),) + pieces[0].shape, jnp.bfloat16),
                pltpu.VMEM((chunk // TILE, rows, TILE), jnp.float32),
                pltpu.SemaphoreType.DMA((len(pieces),)),
            ],
        ),
        out_shape=jax.ShapeDtypeStruct((count, rows, chunk), jnp.bfloat16),
        compiler_params=pltpu.CompilerParams(vmem_limit_bytes=VMEM),
        cost_estimate=pl.CostEstimate(
            flops=2 * tiles.shape[0] * rows * TILE * TILE,
            bytes_accessed=8 * 1024 * 1024,
            transcendentals=0,
        ),
        name="cycle",
    )(slots, blocks, targets, chunks, ladder, tiles, *pieces)


def per_device(
    sec_count,
    inner_count,
    amplitudes,
    hole_ladder,
    bare_integrals,
    ladder_tiles,
    ladder_source,
    ladder_target,
    ladder_live,
    cycle_tiles,
    cycle_source,
    cycle_target,
    gap_rows,
    gap_columns,
):
    rows, _, width = amplitudes.shape
    owned = bare_integrals.shape[2]
    n = sec_count
    z = lax.axis_index("sec")
    me = lax.axis_index("inner")
    amps = amplitudes.reshape(rows, width)

    held = {0: amps[:, :PANEL]}
    bit = inner_count // 2
    while bit:
        pairs = [(i, i ^ bit) for i in range(inner_count)]
        for j in list(held):
            held[j ^ bit] = lax.ppermute(held[j], "inner", pairs)
        bit //= 2
    pieces = [held[j] for j in range(inner_count)]
    panel_blocks = PANEL // TILE
    source = cycle_source[:, 0]
    slots = jnp.bitwise_xor(source // panel_blocks, me)
    blocks = source % panel_blocks
    targets = cycle_target[:, 0]

    ladder = ladder_term(
        amps, ladder_tiles, ladder_source[:, 0], ladder_target[:, 0], ladder_live[:, 0], n
    )
    finish = functools.partial(add_cycle, ladder, cycle_tiles, pieces, slots, blocks, targets)
    edge = jnp.where(z == 0, n - 1, 0).astype(jnp.int32)
    first_share = finish(edge[None])[0]
    shares = finish(jnp.arange(n, dtype=jnp.int32))

    cut = rows // PIECES
    parts = [slice(p * cut, (p + 1) * cut) for p in range(PIECES)]

    def share(index, p):
        picked = lax.dynamic_slice(shares, (jnp.clip(index, 0, n - 1), p * cut, 0), (1, cut, owned))
        return picked[0]

    def plus(a, b):
        return (a.astype(jnp.float32) + b.astype(jnp.float32)).astype(jnp.bfloat16)

    going_up, going_down = [None] * PIECES, [None] * PIECES
    for t in range(1, n):
        up_pairs = [(i, i + 1) for i in range(t)]
        down_pairs = [(n - 1 - i, n - 2 - i) for i in range(t)]
        for p in range(PIECES):
            if t == 1:
                up = down = first_share[parts[p]]
            else:
                up = plus(share(n - t + z, p), going_up[p])
                down = plus(share(t - n + z, p), going_down[p])
            going_up[p] = lax.ppermute(up, "sec", up_pairs)
            going_down[p] = lax.ppermute(down, "sec", down_pairs)

    owned_amps = lax.dynamic_slice(amps, (0, z * owned), (rows, owned))
    hole = jnp.dot(
        hole_ladder,
        lax.all_gather(owned_amps, "row", axis=0, tiled=True),
        preferred_element_type=jnp.float32,
    )
    own = lax.dynamic_index_in_dim(shares, z, 0, keepdims=False)
    base = bare_integrals[:, 0, :].astype(jnp.float32) + hole + own.astype(jnp.float32)
    joined = [
        going_up[p].astype(jnp.float32) + going_down[p].astype(jnp.float32) for p in range(PIECES)
    ]
    residual = base + jnp.concatenate(joined, axis=0)
    denominator = (gap_rows[:, None] + gap_columns[0][None, :]).astype(jnp.float32) / 1024.0
    updated = (residual / denominator).astype(jnp.bfloat16)
    return updated.reshape(rows, 1, owned)


def solution(mesh):
    in_specs = (
        P("row", "inner", None),
        P("row", None),
        P("row", "inner", "sec"),
        P("sec", "inner", None),
        P("sec", "inner"),
        P("sec", "inner"),
        P("sec", "inner"),
        P("sec", "inner", None),
        P("sec", "inner"),
        P("sec", "inner"),
        P("row"),
        P("inner", "sec"),
    )
    return jax.shard_map(
        functools.partial(per_device, mesh.shape["sec"], mesh.shape["inner"]),
        mesh=mesh,
        in_specs=in_specs,
        out_specs=P("row", "inner", "sec"),
        check_vma=False,
    )
```

```python
import functools

import jax
import jax.numpy as jnp
from jax import lax
from jax.experimental import pallas as pl
from jax.experimental.pallas import tpu as pltpu
from jax.sharding import PartitionSpec as P

TILE = 128
PANEL = 2048
GROUP = 32
UNROLL = 8
PIECES = 2
VMEM = 60 * 1024 * 1024


def ladder_kernel(sources, targets, live, amps, tiles, out, acc):
    step = pl.program_id(0)
    blocks_per_chunk = out.shape[2] // TILE

    @pl.when(step == 0)
    def _():
        @pl.loop(0, acc.shape[0])
        def _(b):
            acc[b] = jnp.zeros(acc.shape[1:], jnp.float32)

    here = jnp.clip(live[0] - step * tiles.shape[0], 0, tiles.shape[0])

    def product(t):
        s = pl.multiple_of(sources[step * tiles.shape[0] + t] * TILE, TILE)
        return jnp.dot(amps[:, pl.ds(s, TILE)], tiles[t], preferred_element_type=jnp.float32)

    def add(t, value):
        b = targets[step * tiles.shape[0] + t]
        acc[b] = acc[b] + value

    full = here // UNROLL

    @pl.loop(0, full)
    def _(g):
        values = [product(g * UNROLL + u) for u in range(UNROLL)]
        for u in range(UNROLL):
            add(g * UNROLL + u, values[u])

    @pl.loop(full * UNROLL, here)
    def _(t):
        add(t, product(t))

    @pl.when(step == pl.num_programs(0) - 1)
    def _():
        for c in range(out.shape[0]):

            @pl.loop(0, blocks_per_chunk)
            def _(b):
                columns = pl.ds(pl.multiple_of(b * TILE, TILE), TILE)
                out[c, :, columns] = acc[c * blocks_per_chunk + b].astype(out.dtype)


def ladder_term(amps, tiles, sources, targets, live, chunk_count):
    rows, width = amps.shape
    count = tiles.shape[0]
    group = GROUP if count % GROUP == 0 else count
    chunk = width // chunk_count
    return pl.pallas_call(
        ladder_kernel,
        grid_spec=pltpu.PrefetchScalarGridSpec(
            num_scalar_prefetch=3,
            grid=(count // group,),
            in_specs=[
                pl.BlockSpec((rows, width), lambda g, s, t, n: (0, 0)),
                pl.BlockSpec(
                    (group, TILE, TILE),
                    lambda g, s, t, n: (jnp.minimum(g, jnp.maximum(n[0] - 1, 0) // group), 0, 0),
                ),
            ],
            out_specs=pl.BlockSpec((chunk_count, rows, chunk), lambda g, s, t, n: (0, 0, 0)),
            scratch_shapes=[pltpu.VMEM((width // TILE, rows, TILE), jnp.float32)],
        ),
        out_shape=jax.ShapeDtypeStruct((chunk_count, rows, chunk), jnp.bfloat16),
        compiler_params=pltpu.CompilerParams(vmem_limit_bytes=VMEM),
        cost_estimate=pl.CostEstimate(
            flops=8 * count * rows * TILE * TILE, bytes_accessed=40 * 1024 * 1024, transcendentals=0
        ),
        name="ladder",
    )(sources, targets, live, amps, tiles)


def cycle_kernel(slots, blocks, targets, chunks, ladder, tiles, *rest):
    panel, acc, sems = rest[-3:]
    outs = rest[-3 - PIECES : -3]
    pieces = rest[: -3 - PIECES]
    step = pl.program_id(0)
    blocks_per_chunk = acc.shape[0]
    first = chunks[step] * blocks_per_chunk
    copies = [pltpu.make_async_copy(p, panel.at[j], sems.at[j]) for j, p in enumerate(pieces)]

    @pl.when(step == 0)
    def _():
        for copy in copies:
            copy.start()

    @pl.loop(0, blocks_per_chunk)
    def _(b):
        columns = pl.ds(pl.multiple_of(b * TILE, TILE), TILE)
        acc[b] = ladder[0, :, columns].astype(jnp.float32)

    @pl.when(step == 0)
    def _():
        for copy in copies:
            copy.wait()

    @pl.loop(0, tiles.shape[0])
    def _(t):
        b = targets[t] - first

        @pl.when((b >= 0) & (b < blocks_per_chunk))
        def _():
            columns = pl.ds(pl.multiple_of(blocks[t] * TILE, TILE), TILE)
            acc[b] = acc[b] + jnp.dot(
                panel[slots[t], :, columns], tiles[t], preferred_element_type=jnp.float32
            )

    @pl.loop(0, blocks_per_chunk)
    def _(b):
        columns = pl.ds(pl.multiple_of(b * TILE, TILE), TILE)
        value = acc[b].astype(outs[0].dtype)
        cut = outs[0].shape[1]
        for p in range(PIECES):
            outs[p][0, :, columns] = value[p * cut : (p + 1) * cut]


def add_cycle(ladder, tiles, pieces, slots, blocks, targets, chunks):
    _, rows, chunk = ladder.shape
    count = chunks.shape[0]
    return pl.pallas_call(
        cycle_kernel,
        grid_spec=pltpu.PrefetchScalarGridSpec(
            num_scalar_prefetch=4,
            grid=(count,),
            in_specs=[
                pl.BlockSpec((1, rows, chunk), lambda i, s, b, t, c: (c[i], 0, 0)),
                pl.BlockSpec(tiles.shape, lambda i, s, b, t, c: (0, 0, 0)),
            ]
            + [pl.BlockSpec(memory_space=pl.ANY)] * len(pieces),
            out_specs=[pl.BlockSpec((1, rows // PIECES, chunk), lambda i, s, b, t, c: (i, 0, 0))]
            * PIECES,
            scratch_shapes=[
                pltpu.VMEM((len(pieces),) + pieces[0].shape, jnp.bfloat16),
                pltpu.VMEM((chunk // TILE, rows, TILE), jnp.float32),
                pltpu.SemaphoreType.DMA((len(pieces),)),
            ],
        ),
        out_shape=[jax.ShapeDtypeStruct((count, rows // PIECES, chunk), jnp.bfloat16)] * PIECES,
        compiler_params=pltpu.CompilerParams(vmem_limit_bytes=VMEM),
        cost_estimate=pl.CostEstimate(
            flops=2 * tiles.shape[0] * rows * TILE * TILE,
            bytes_accessed=8 * 1024 * 1024,
            transcendentals=0,
        ),
        name="cycle",
    )(slots, blocks, targets, chunks, ladder, tiles, *pieces)


def per_device(
    sec_count,
    inner_count,
    amplitudes,
    hole_ladder,
    bare_integrals,
    ladder_tiles,
    ladder_source,
    ladder_target,
    ladder_live,
    cycle_tiles,
    cycle_source,
    cycle_target,
    gap_rows,
    gap_columns,
):
    rows, _, width = amplitudes.shape
    owned = bare_integrals.shape[2]
    n = sec_count
    z = lax.axis_index("sec")
    me = lax.axis_index("inner")
    amps = amplitudes.reshape(rows, width)

    owned_amps = lax.dynamic_slice(amps, (0, z * owned), (rows, owned))
    owned_all = lax.all_gather(owned_amps, "row", axis=0, tiled=True)

    ladder = ladder_term(
        amps, ladder_tiles, ladder_source[:, 0], ladder_target[:, 0], ladder_live[:, 0], n
    )

    held = {0: amps[:, :PANEL]}
    bit = inner_count // 2
    while bit:
        pairs = [(i, i ^ bit) for i in range(inner_count)]
        for j in list(held):
            held[j ^ bit] = lax.ppermute(held[j], "inner", pairs)
        if bit == inner_count // 2 and bit > 1:
            held[bit], ladder = lax.optimization_barrier((held[bit], ladder))
        bit //= 2
    pieces = [held[j] for j in range(inner_count)]
    panel_blocks = PANEL // TILE
    source = cycle_source[:, 0]
    slots = jnp.bitwise_xor(source // panel_blocks, me)
    blocks = source % panel_blocks
    targets = cycle_target[:, 0]

    finish = functools.partial(add_cycle, ladder, cycle_tiles, pieces, slots, blocks, targets)
    edge = jnp.where(z == 0, n - 1, 0).astype(jnp.int32)
    first_shares = finish(edge[None])
    shares = finish(jnp.arange(n, dtype=jnp.int32))

    hole = jnp.dot(hole_ladder, owned_all, preferred_element_type=jnp.float32)
    base = bare_integrals[:, 0, :].astype(jnp.float32) + hole

    def share(index, p):
        return lax.dynamic_index_in_dim(shares[p], jnp.clip(index, 0, n - 1), 0, keepdims=False)

    def plus(a, b):
        return (a.astype(jnp.float32) + b.astype(jnp.float32)).astype(jnp.bfloat16)

    going = [None] * PIECES
    for t in range(1, n):
        up_pairs = [(i, i + 1) for i in range(t)]
        down_pairs = [(n - 1 - i, n - 2 - i) for i in range(t)]
        for p in range(PIECES):
            if t == 1:
                up = down = first_shares[p][0]
            elif 2 * t <= n:
                up = down = share(jnp.where(z < t, n - t + z, t - n + z), p)
                if len(going[p]) == 1:
                    up = down = plus(up, going[p][0])
                else:
                    up = down = plus(up, jnp.where(z < t, going[p][0], going[p][1]))
            else:
                up = plus(share(n - t + z, p), going[p][0])
                down = plus(share(t - n + z, p), going[p][-1])
            if 2 * t < n - 1:
                going[p] = [lax.ppermute(up, "sec", up_pairs + down_pairs)]
            else:
                going[p] = [
                    lax.ppermute(up, "sec", up_pairs),
                    lax.ppermute(down, "sec", down_pairs),
                ]
            if t == 1 and p == PIECES - 1:
                going[0][0], base = lax.optimization_barrier((going[0][0], base))

    joined = [
        share(z, p).astype(jnp.float32) + sum(g.astype(jnp.float32) for g in going[p])
        for p in range(PIECES)
    ]
    residual = base + jnp.concatenate(joined, axis=0)
    denominator = (gap_rows[:, None] + gap_columns[0][None, :]).astype(jnp.float32) / 1024.0
    updated = (residual / denominator).astype(jnp.bfloat16)
    return updated.reshape(rows, 1, owned)


def solution(mesh):
    in_specs = (
        P("row", "inner", None),
        P("row", None),
        P("row", "inner", "sec"),
        P("sec", "inner", None),
        P("sec", "inner"),
        P("sec", "inner"),
        P("sec", "inner"),
        P("sec", "inner", None),
        P("sec", "inner"),
        P("sec", "inner"),
        P("row"),
        P("inner", "sec"),
    )
    return jax.shard_map(
        functools.partial(per_device, mesh.shape["sec"], mesh.shape["inner"]),
        mesh=mesh,
        in_specs=in_specs,
        out_specs=P("row", "inner", "sec"),
        check_vma=False,
    )
```

```python
import functools

import jax
import jax.numpy as jnp
from jax import lax
from jax.experimental import pallas as pl
from jax.experimental.pallas import tpu as pltpu
from jax.sharding import PartitionSpec as P

TILE = 128
PANEL = 2048
GROUP = 32
UNROLL = 8
PIECES = 2
VMEM = 60 * 1024 * 1024


def ladder_kernel(sources, targets, live, place, amps, tiles, out, own, acc):
    step = pl.program_id(0)
    blocks_per_chunk = out.shape[2] // TILE

    @pl.when(step == 0)
    def _():
        @pl.loop(0, acc.shape[0], unroll=4)
        def _(b):
            acc[b] = jnp.zeros(acc.shape[1:], jnp.float32)

        start = place[0] * blocks_per_chunk

        @pl.loop(0, blocks_per_chunk, unroll=4)
        def _(b):
            columns = pl.ds(pl.multiple_of(b * TILE, TILE), TILE)
            own[:, columns] = amps[:, pl.ds(pl.multiple_of((start + b) * TILE, TILE), TILE)]

    here = jnp.clip(live[0] - step * tiles.shape[0], 0, tiles.shape[0])

    def product(t):
        s = pl.multiple_of(sources[step * tiles.shape[0] + t] * TILE, TILE)
        return jnp.dot(amps[:, pl.ds(s, TILE)], tiles[t], preferred_element_type=jnp.float32)

    def add(t, value):
        b = targets[step * tiles.shape[0] + t]
        acc[b] = acc[b] + value

    full = here // UNROLL

    @pl.loop(0, full)
    def _(g):
        values = [product(g * UNROLL + u) for u in range(UNROLL)]
        for u in range(UNROLL):
            add(g * UNROLL + u, values[u])

    @pl.loop(full * UNROLL, here)
    def _(t):
        add(t, product(t))

    @pl.when(step == pl.num_programs(0) - 1)
    def _():
        for c in range(out.shape[0]):

            @pl.loop(0, blocks_per_chunk, unroll=4)
            def _(b):
                columns = pl.ds(pl.multiple_of(b * TILE, TILE), TILE)
                out[c, :, columns] = acc[c * blocks_per_chunk + b].astype(out.dtype)


def ladder_term(amps, tiles, sources, targets, live, place, chunk_count):
    rows, width = amps.shape
    count = tiles.shape[0]
    group = GROUP if count % GROUP == 0 else count
    chunk = width // chunk_count
    return pl.pallas_call(
        ladder_kernel,
        grid_spec=pltpu.PrefetchScalarGridSpec(
            num_scalar_prefetch=4,
            grid=(count // group,),
            in_specs=[
                pl.BlockSpec((rows, width), lambda g, s, t, n, z: (0, 0)),
                pl.BlockSpec(
                    (group, TILE, TILE),
                    lambda g, s, t, n, z: (jnp.minimum(g, jnp.maximum(n[0] - 1, 0) // group), 0, 0),
                ),
            ],
            out_specs=[
                pl.BlockSpec((chunk_count, rows, chunk), lambda g, s, t, n, z: (0, 0, 0)),
                pl.BlockSpec((rows, chunk), lambda g, s, t, n, z: (0, 0)),
            ],
            scratch_shapes=[pltpu.VMEM((width // TILE, rows, TILE), jnp.float32)],
        ),
        out_shape=[
            jax.ShapeDtypeStruct((chunk_count, rows, chunk), jnp.bfloat16),
            jax.ShapeDtypeStruct((rows, chunk), jnp.bfloat16),
        ],
        compiler_params=pltpu.CompilerParams(vmem_limit_bytes=VMEM),
        cost_estimate=pl.CostEstimate(
            flops=8 * count * rows * TILE * TILE, bytes_accessed=40 * 1024 * 1024, transcendentals=0
        ),
        name="ladder",
    )(sources, targets, live, place, amps, tiles)


def cycle_kernel(slots, blocks, targets, chunks, ladder, tiles, *rest):
    panel, acc, sems = rest[-3:]
    outs = rest[-3 - PIECES : -3]
    pieces = rest[: -3 - PIECES]
    step = pl.program_id(0)
    blocks_per_chunk = acc.shape[0] - 1
    first = chunks[step] * blocks_per_chunk
    copies = [pltpu.make_async_copy(p, panel.at[j], sems.at[j]) for j, p in enumerate(pieces)]

    @pl.when(step == 0)
    def _():
        for copy in copies:
            copy.start()

    @pl.loop(0, blocks_per_chunk, unroll=4)
    def _(b):
        columns = pl.ds(pl.multiple_of(b * TILE, TILE), TILE)
        acc[b] = ladder[0, :, columns].astype(jnp.float32)

    @pl.when(step == 0)
    def _():
        for copy in copies:
            copy.wait()

    def product(t):
        columns = pl.ds(pl.multiple_of(blocks[t] * TILE, TILE), TILE)
        return jnp.dot(panel[slots[t], :, columns], tiles[t], preferred_element_type=jnp.float32)

    def add(t, value):
        b = targets[t] - first
        b = jnp.where((b >= 0) & (b < blocks_per_chunk), b, blocks_per_chunk)
        acc[b] = acc[b] + value

    unroll = UNROLL if tiles.shape[0] % UNROLL == 0 else 1

    @pl.loop(0, tiles.shape[0] // unroll)
    def _(g):
        values = [product(g * unroll + u) for u in range(unroll)]
        for u in range(unroll):
            add(g * unroll + u, values[u])

    @pl.loop(0, blocks_per_chunk, unroll=4)
    def _(b):
        columns = pl.ds(pl.multiple_of(b * TILE, TILE), TILE)
        value = acc[b].astype(outs[0].dtype)
        cut = outs[0].shape[1]
        for p in range(PIECES):
            outs[p][0, :, columns] = value[p * cut : (p + 1) * cut]


def add_cycle(ladder, tiles, pieces, slots, blocks, targets, chunks):
    _, rows, chunk = ladder.shape
    count = chunks.shape[0]
    return pl.pallas_call(
        cycle_kernel,
        grid_spec=pltpu.PrefetchScalarGridSpec(
            num_scalar_prefetch=4,
            grid=(count,),
            in_specs=[
                pl.BlockSpec((1, rows, chunk), lambda i, s, b, t, c: (c[i], 0, 0)),
                pl.BlockSpec(tiles.shape, lambda i, s, b, t, c: (0, 0, 0)),
            ]
            + [pl.BlockSpec(memory_space=pl.ANY)] * len(pieces),
            out_specs=[pl.BlockSpec((1, rows // PIECES, chunk), lambda i, s, b, t, c: (i, 0, 0))]
            * PIECES,
            scratch_shapes=[
                pltpu.VMEM((len(pieces),) + pieces[0].shape, jnp.bfloat16),
                pltpu.VMEM((chunk // TILE + 1, rows, TILE), jnp.float32),
                pltpu.SemaphoreType.DMA((len(pieces),)),
            ],
        ),
        out_shape=[jax.ShapeDtypeStruct((count, rows // PIECES, chunk), jnp.bfloat16)] * PIECES,
        compiler_params=pltpu.CompilerParams(vmem_limit_bytes=VMEM),
        cost_estimate=pl.CostEstimate(
            flops=2 * tiles.shape[0] * rows * TILE * TILE,
            bytes_accessed=8 * 1024 * 1024,
            transcendentals=0,
        ),
        name="cycle",
    )(slots, blocks, targets, chunks, ladder, tiles, *pieces)


def per_device(
    sec_count,
    inner_count,
    amplitudes,
    hole_ladder,
    bare_integrals,
    ladder_tiles,
    ladder_source,
    ladder_target,
    ladder_live,
    cycle_tiles,
    cycle_source,
    cycle_target,
    gap_rows,
    gap_columns,
):
    rows, _, width = amplitudes.shape
    owned = bare_integrals.shape[2]
    n = sec_count
    z = lax.axis_index("sec")
    me = lax.axis_index("inner")
    amps = amplitudes.reshape(rows, width)

    ladder, owned_amps = ladder_term(
        amps,
        ladder_tiles,
        ladder_source[:, 0],
        ladder_target[:, 0],
        ladder_live[:, 0],
        z[None],
        n,
    )
    owned_all = lax.all_gather(owned_amps, "row", axis=0, tiled=True)

    held = {0: amps[:, :PANEL]}
    bit = inner_count // 2
    while bit:
        pairs = [(i, i ^ bit) for i in range(inner_count)]
        for j in list(held):
            held[j ^ bit] = lax.ppermute(held[j], "inner", pairs)
        if bit == inner_count // 2 and bit > 1:
            held[bit], ladder = lax.optimization_barrier((held[bit], ladder))
        bit //= 2
    pieces = [held[j] for j in range(inner_count)]
    panel_blocks = PANEL // TILE
    source = cycle_source[:, 0]
    slots = jnp.bitwise_xor(source // panel_blocks, me)
    blocks = source % panel_blocks
    targets = cycle_target[:, 0]

    finish = functools.partial(add_cycle, ladder, cycle_tiles, pieces, slots, blocks, targets)
    edge = jnp.where(z == 0, n - 1, 0).astype(jnp.int32)
    first_shares = finish(edge[None])
    shares = finish(jnp.arange(n, dtype=jnp.int32))

    hole = jnp.dot(hole_ladder, owned_all, preferred_element_type=jnp.float32)
    base = bare_integrals[:, 0, :].astype(jnp.float32) + hole

    def share(index, p):
        return lax.dynamic_index_in_dim(shares[p], jnp.clip(index, 0, n - 1), 0, keepdims=False)

    def plus(a, b):
        return (a.astype(jnp.float32) + b.astype(jnp.float32)).astype(jnp.bfloat16)

    going = [None] * PIECES
    for t in range(1, n):
        up_pairs = [(i, i + 1) for i in range(t)]
        down_pairs = [(n - 1 - i, n - 2 - i) for i in range(t)]
        for p in range(PIECES):
            if t == 1:
                up = down = first_shares[p][0]
            elif 2 * t <= n:
                up = down = share(jnp.where(z < t, n - t + z, t - n + z), p)
                if len(going[p]) == 1:
                    up = down = plus(up, going[p][0])
                else:
                    up = down = plus(up, jnp.where(z < t, going[p][0], going[p][1]))
            else:
                up = plus(share(n - t + z, p), going[p][0])
                down = plus(share(t - n + z, p), going[p][-1])
            if 2 * t < n - 1:
                going[p] = [lax.ppermute(up, "sec", up_pairs + down_pairs)]
            else:
                going[p] = [
                    lax.ppermute(up, "sec", up_pairs),
                    lax.ppermute(down, "sec", down_pairs),
                ]
            if t == 1 and p == PIECES - 1:
                going[0][0], base = lax.optimization_barrier((going[0][0], base))

    joined = [
        share(z, p).astype(jnp.float32) + sum(g.astype(jnp.float32) for g in going[p])
        for p in range(PIECES)
    ]
    residual = base + jnp.concatenate(joined, axis=0)
    denominator = (gap_rows[:, None] + gap_columns[0][None, :]).astype(jnp.float32) / 1024.0
    updated = (residual / denominator).astype(jnp.bfloat16)
    return updated.reshape(rows, 1, owned)


def solution(mesh):
    in_specs = (
        P("row", "inner", None),
        P("row", None),
        P("row", "inner", "sec"),
        P("sec", "inner", None),
        P("sec", "inner"),
        P("sec", "inner"),
        P("sec", "inner"),
        P("sec", "inner", None),
        P("sec", "inner"),
        P("sec", "inner"),
        P("row"),
        P("inner", "sec"),
    )
    return jax.shard_map(
        functools.partial(per_device, mesh.shape["sec"], mesh.shape["inner"]),
        mesh=mesh,
        in_specs=in_specs,
        out_specs=P("row", "inner", "sec"),
        check_vma=False,
    )
```

```python
import functools

import jax
import jax.numpy as jnp
from jax import lax
from jax.experimental import pallas as pl
from jax.experimental.pallas import tpu as pltpu
from jax.sharding import PartitionSpec as P

TILE = 128
PANEL = 2048
GROUP = 32
UNROLL = 8
PIECES = 2
VMEM = 60 * 1024 * 1024


def ladder_kernel(
    sources, targets, live, place, amps_in, tiles, out_all, own, amps, out, acc, in_sem, out_sems
):
    step = pl.program_id(0)
    fetch = pltpu.make_async_copy(amps_in, amps, in_sem)
    blocks_per_chunk = out.shape[2] // TILE

    @pl.when(step == 0)
    def _():
        fetch.start()

        @pl.loop(0, acc.shape[0], unroll=4)
        def _(b):
            acc[b] = jnp.zeros(acc.shape[1:], jnp.float32)

        fetch.wait()
        start = place[0] * blocks_per_chunk

        @pl.loop(0, blocks_per_chunk, unroll=4)
        def _(b):
            columns = pl.ds(pl.multiple_of(b * TILE, TILE), TILE)
            own[:, columns] = amps[:, pl.ds(pl.multiple_of((start + b) * TILE, TILE), TILE)]

    here = jnp.clip(live[0] - step * tiles.shape[0], 0, tiles.shape[0])

    def product(t):
        s = pl.multiple_of(sources[step * tiles.shape[0] + t] * TILE, TILE)
        return jnp.dot(amps[:, pl.ds(s, TILE)], tiles[t], preferred_element_type=jnp.float32)

    def add(t, value):
        b = targets[step * tiles.shape[0] + t]
        acc[b] = acc[b] + value

    full = here // UNROLL

    @pl.loop(0, full)
    def _(g):
        values = [product(g * UNROLL + u) for u in range(UNROLL)]
        for u in range(UNROLL):
            add(g * UNROLL + u, values[u])

    @pl.loop(full * UNROLL, here)
    def _(t):
        add(t, product(t))

    @pl.when(step == pl.num_programs(0) - 1)
    def _():
        writes = []
        for c in range(out.shape[0]):

            @pl.loop(0, blocks_per_chunk, unroll=4)
            def _(b):
                columns = pl.ds(pl.multiple_of(b * TILE, TILE), TILE)
                out[c, :, columns] = acc[c * blocks_per_chunk + b].astype(out.dtype)

            writes.append(pltpu.make_async_copy(out.at[c], out_all.at[c], out_sems.at[c]))
            writes[c].start()
        for write in writes:
            write.wait()


def ladder_term(amps, tiles, sources, targets, live, place, chunk_count):
    rows, width = amps.shape
    count = tiles.shape[0]
    group = GROUP if count % GROUP == 0 else count
    chunk = width // chunk_count
    return pl.pallas_call(
        ladder_kernel,
        grid_spec=pltpu.PrefetchScalarGridSpec(
            num_scalar_prefetch=4,
            grid=(count // group,),
            in_specs=[
                pl.BlockSpec(memory_space=pl.ANY),
                pl.BlockSpec(
                    (group, TILE, TILE),
                    lambda g, s, t, n, z: (jnp.minimum(g, jnp.maximum(n[0] - 1, 0) // group), 0, 0),
                ),
            ],
            out_specs=[
                pl.BlockSpec(memory_space=pl.ANY),
                pl.BlockSpec((rows, chunk), lambda g, s, t, n, z: (0, 0)),
            ],
            scratch_shapes=[
                pltpu.VMEM((rows, width), jnp.bfloat16),
                pltpu.VMEM((chunk_count, rows, chunk), jnp.bfloat16),
                pltpu.VMEM((width // TILE, rows, TILE), jnp.float32),
                pltpu.SemaphoreType.DMA,
                pltpu.SemaphoreType.DMA((chunk_count,)),
            ],
        ),
        out_shape=[
            jax.ShapeDtypeStruct((chunk_count, rows, chunk), jnp.bfloat16),
            jax.ShapeDtypeStruct((rows, chunk), jnp.bfloat16),
        ],
        compiler_params=pltpu.CompilerParams(vmem_limit_bytes=VMEM),
        cost_estimate=pl.CostEstimate(
            flops=8 * count * rows * TILE * TILE, bytes_accessed=40 * 1024 * 1024, transcendentals=0
        ),
        name="ladder",
    )(sources, targets, live, place, amps, tiles)


def cycle_kernel(part, outputs, slots, blocks, targets, chunks, ladder, tiles_in, *rest):
    panel, tiles, acc, tile_sem, sems = rest[-5:]
    outs = rest[-5 - outputs : -5]
    pieces = rest[: -5 - outputs]
    step = pl.program_id(0)
    blocks_per_chunk = acc.shape[0] - 1
    first = chunks[step] * blocks_per_chunk
    rows = panel.shape[1]
    copies = [pltpu.make_async_copy(tiles_in, tiles, tile_sem)] + [
        pltpu.make_async_copy(p.at[pl.ds(part * rows, rows)], panel.at[j], sems.at[j])
        for j, p in enumerate(pieces)
    ]

    @pl.when(step == 0)
    def _():
        for copy in copies:
            copy.start()

    @pl.loop(0, blocks_per_chunk, unroll=4)
    def _(b):
        columns = pl.ds(pl.multiple_of(b * TILE, TILE), TILE)
        acc[b] = ladder[0, :, columns].astype(jnp.float32)

    @pl.when(step == 0)
    def _():
        for copy in copies:
            copy.wait()

    def product(t):
        columns = pl.ds(pl.multiple_of(blocks[t] * TILE, TILE), TILE)
        return jnp.dot(panel[slots[t], :, columns], tiles[t], preferred_element_type=jnp.float32)

    def add(t, value):
        b = targets[t] - first
        b = jnp.where((b >= 0) & (b < blocks_per_chunk), b, blocks_per_chunk)
        acc[b] = acc[b] + value

    unroll = UNROLL if tiles.shape[0] % UNROLL == 0 else 1

    @pl.loop(0, tiles.shape[0] // unroll)
    def _(g):
        values = [product(g * unroll + u) for u in range(unroll)]
        for u in range(unroll):
            add(g * unroll + u, values[u])

    @pl.loop(0, blocks_per_chunk, unroll=4)
    def _(b):
        columns = pl.ds(pl.multiple_of(b * TILE, TILE), TILE)
        value = acc[b].astype(outs[0].dtype)
        cut = outs[0].shape[1]
        for p in range(outputs):
            outs[p][0, :, columns] = value[p * cut : (p + 1) * cut]


def add_cycle(ladder, tiles, pieces, slots, blocks, targets, chunks, part=None):
    _, rows, chunk = ladder.shape
    count = chunks.shape[0]
    cut = rows // PIECES
    outputs = PIECES if part is None else 1
    if part is None:
        part = 0
    else:
        rows = cut
    return pl.pallas_call(
        functools.partial(cycle_kernel, part, outputs),
        grid_spec=pltpu.PrefetchScalarGridSpec(
            num_scalar_prefetch=4,
            grid=(count,),
            in_specs=[pl.BlockSpec((1, rows, chunk), lambda i, s, b, t, c: (c[i], part, 0))]
            + [pl.BlockSpec(memory_space=pl.ANY)] * (1 + len(pieces)),
            out_specs=[pl.BlockSpec((1, cut, chunk), lambda i, s, b, t, c: (i, 0, 0))] * outputs,
            scratch_shapes=[
                pltpu.VMEM((len(pieces), rows, pieces[0].shape[1]), jnp.bfloat16),
                pltpu.VMEM(tiles.shape, jnp.bfloat16),
                pltpu.VMEM((chunk // TILE + 1, rows, TILE), jnp.float32),
                pltpu.SemaphoreType.DMA,
                pltpu.SemaphoreType.DMA((len(pieces),)),
            ],
        ),
        out_shape=[jax.ShapeDtypeStruct((count, cut, chunk), jnp.bfloat16)] * outputs,
        compiler_params=pltpu.CompilerParams(vmem_limit_bytes=VMEM),
        cost_estimate=pl.CostEstimate(
            flops=2 * tiles.shape[0] * rows * TILE * TILE,
            bytes_accessed=8 * 1024 * 1024,
            transcendentals=0,
        ),
        name="cycle",
    )(slots, blocks, targets, chunks, ladder, tiles, *pieces)


def per_device(
    sec_count,
    inner_count,
    amplitudes,
    hole_ladder,
    bare_integrals,
    ladder_tiles,
    ladder_source,
    ladder_target,
    ladder_live,
    cycle_tiles,
    cycle_source,
    cycle_target,
    gap_rows,
    gap_columns,
):
    rows, _, width = amplitudes.shape
    owned = bare_integrals.shape[2]
    n = sec_count
    z = lax.axis_index("sec")
    me = lax.axis_index("inner")
    amps = amplitudes.reshape(rows, width)

    ladder, owned_amps = ladder_term(
        amps,
        ladder_tiles,
        ladder_source[:, 0],
        ladder_target[:, 0],
        ladder_live[:, 0],
        z[None],
        n,
    )
    owned_all = lax.all_gather(owned_amps, "row", axis=0, tiled=True)

    held = {0: amps[:, :PANEL]}
    bit = inner_count // 2
    while bit:
        pairs = [(i, i ^ bit) for i in range(inner_count)]
        for j in list(held):
            held[j ^ bit] = lax.ppermute(held[j], "inner", pairs)
        if bit == inner_count // 2 and bit > 1:
            held[bit], ladder = lax.optimization_barrier((held[bit], ladder))
        bit //= 2
    pieces = [held[j] for j in range(inner_count)]
    panel_blocks = PANEL // TILE
    source = cycle_source[:, 0]
    slots = jnp.bitwise_xor(source // panel_blocks, me)
    blocks = source % panel_blocks
    targets = cycle_target[:, 0]

    finish = functools.partial(add_cycle, ladder, cycle_tiles, pieces, slots, blocks, targets)
    edge = jnp.where(z == 0, n - 1, 0).astype(jnp.int32)
    first_shares = [finish(edge[None], part=p)[0] for p in range(PIECES)]
    shares = finish(jnp.arange(n, dtype=jnp.int32))

    hole = jnp.dot(hole_ladder, owned_all, preferred_element_type=jnp.float32)
    base = bare_integrals[:, 0, :].astype(jnp.float32) + hole

    def share(index, p):
        return lax.dynamic_index_in_dim(shares[p], jnp.clip(index, 0, n - 1), 0, keepdims=False)

    def plus(a, b):
        return (a.astype(jnp.float32) + b.astype(jnp.float32)).astype(jnp.bfloat16)

    going = [None] * PIECES
    for t in range(1, n):
        up_pairs = [(i, i + 1) for i in range(t)]
        down_pairs = [(n - 1 - i, n - 2 - i) for i in range(t)]
        for p in range(PIECES):
            if t == 1:
                up = down = first_shares[p][0]
            elif 2 * t <= n:
                up = down = share(jnp.where(z < t, n - t + z, t - n + z), p)
                if len(going[p]) == 1:
                    up = down = plus(up, going[p][0])
                else:
                    up = down = plus(up, jnp.where(z < t, going[p][0], going[p][1]))
            else:
                up = plus(share(n - t + z, p), going[p][0])
                down = plus(share(t - n + z, p), going[p][-1])
            if 2 * t < n - 1:
                going[p] = [lax.ppermute(up, "sec", up_pairs + down_pairs)]
            else:
                going[p] = [
                    lax.ppermute(up, "sec", up_pairs),
                    lax.ppermute(down, "sec", down_pairs),
                ]
            if t == 1 and p == PIECES - 1:
                going[0][0], base = lax.optimization_barrier((going[0][0], base))

    joined = [
        share(z, p).astype(jnp.float32) + sum(g.astype(jnp.float32) for g in going[p])
        for p in range(PIECES)
    ]
    residual = base + jnp.concatenate(joined, axis=0)
    denominator = (gap_rows[:, None] + gap_columns[0][None, :]).astype(jnp.float32) / 1024.0
    updated = (residual / denominator).astype(jnp.bfloat16)
    return updated.reshape(rows, 1, owned)


def solution(mesh):
    in_specs = (
        P("row", "inner", None),
        P("row", None),
        P("row", "inner", "sec"),
        P("sec", "inner", None),
        P("sec", "inner"),
        P("sec", "inner"),
        P("sec", "inner"),
        P("sec", "inner", None),
        P("sec", "inner"),
        P("sec", "inner"),
        P("row"),
        P("inner", "sec"),
    )
    return jax.shard_map(
        functools.partial(per_device, mesh.shape["sec"], mesh.shape["inner"]),
        mesh=mesh,
        in_specs=in_specs,
        out_specs=P("row", "inner", "sec"),
        check_vma=False,
    )
```

```python
import functools

import jax
import jax.numpy as jnp
from jax import lax
from jax.experimental import pallas as pl
from jax.experimental.pallas import tpu as pltpu
from jax.sharding import PartitionSpec as P

TILE = 128
PANEL = 2048
GROUP = 32
UNROLL = 8
PIECES = 2
VMEM = 60 * 1024 * 1024


def ladder_kernel(
    sources, targets, live, place, amps_in, tiles, out_all, own, amps, out, acc, in_sem, out_sems
):
    step = pl.program_id(0)
    fetch = pltpu.make_async_copy(amps_in, amps, in_sem)
    blocks_per_chunk = out.shape[2] // TILE

    @pl.when(step == 0)
    def _():
        fetch.start()

        @pl.loop(0, acc.shape[0], unroll=4)
        def _(b):
            acc[b] = jnp.zeros(acc.shape[1:], jnp.float32)

        fetch.wait()
        start = place[0] * blocks_per_chunk

        @pl.loop(0, blocks_per_chunk, unroll=4)
        def _(b):
            columns = pl.ds(pl.multiple_of(b * TILE, TILE), TILE)
            own[:, columns] = amps[:, pl.ds(pl.multiple_of((start + b) * TILE, TILE), TILE)]

    here = jnp.clip(live[0] - step * tiles.shape[0], 0, tiles.shape[0])

    def product(t):
        s = pl.multiple_of(sources[step * tiles.shape[0] + t] * TILE, TILE)
        return jnp.dot(amps[:, pl.ds(s, TILE)], tiles[t], preferred_element_type=jnp.float32)

    def add(t, value):
        b = targets[step * tiles.shape[0] + t]
        acc[b] = acc[b] + value

    full = here // UNROLL

    @pl.loop(0, full)
    def _(g):
        values = [product(g * UNROLL + u) for u in range(UNROLL)]
        for u in range(UNROLL):
            add(g * UNROLL + u, values[u])

    @pl.loop(full * UNROLL, here)
    def _(t):
        add(t, product(t))

    @pl.when(step == pl.num_programs(0) - 1)
    def _():
        writes = []
        for c in range(out.shape[0]):

            @pl.loop(0, blocks_per_chunk, unroll=4)
            def _(b):
                columns = pl.ds(pl.multiple_of(b * TILE, TILE), TILE)
                out[c, :, columns] = acc[c * blocks_per_chunk + b].astype(out.dtype)

            writes.append(pltpu.make_async_copy(out.at[c], out_all.at[c], out_sems.at[c]))
            writes[c].start()
        for write in writes:
            write.wait()


def ladder_term(amps, tiles, sources, targets, live, place, chunk_count):
    rows, width = amps.shape
    count = tiles.shape[0]
    group = GROUP if count % GROUP == 0 else count
    chunk = width // chunk_count
    return pl.pallas_call(
        ladder_kernel,
        grid_spec=pltpu.PrefetchScalarGridSpec(
            num_scalar_prefetch=4,
            grid=(count // group,),
            in_specs=[
                pl.BlockSpec(memory_space=pl.ANY),
                pl.BlockSpec(
                    (group, TILE, TILE),
                    lambda g, s, t, n, z: (jnp.minimum(g, jnp.maximum(n[0] - 1, 0) // group), 0, 0),
                ),
            ],
            out_specs=[
                pl.BlockSpec(memory_space=pl.ANY),
                pl.BlockSpec((rows, chunk), lambda g, s, t, n, z: (0, 0)),
            ],
            scratch_shapes=[
                pltpu.VMEM((rows, width), jnp.bfloat16),
                pltpu.VMEM((chunk_count, rows, chunk), jnp.bfloat16),
                pltpu.VMEM((width // TILE, rows, TILE), jnp.float32),
                pltpu.SemaphoreType.DMA,
                pltpu.SemaphoreType.DMA((chunk_count,)),
            ],
        ),
        out_shape=[
            jax.ShapeDtypeStruct((chunk_count, rows, chunk), jnp.bfloat16),
            jax.ShapeDtypeStruct((rows, chunk), jnp.bfloat16),
        ],
        compiler_params=pltpu.CompilerParams(vmem_limit_bytes=VMEM),
        cost_estimate=pl.CostEstimate(
            flops=8 * count * rows * TILE * TILE, bytes_accessed=40 * 1024 * 1024, transcendentals=0
        ),
        name="ladder",
    )(sources, targets, live, place, amps, tiles)


def cycle_kernel(part, outputs, slots, blocks, targets, chunks, ladder, tiles_in, *rest):
    panel, tiles, acc, tile_sem, sems = rest[-5:]
    outs = rest[-5 - outputs : -5]
    pieces = rest[: -5 - outputs]
    step = pl.program_id(0)
    blocks_per_chunk = acc.shape[0] - 1
    first = chunks[step] * blocks_per_chunk
    rows = panel.shape[1]
    copies = [pltpu.make_async_copy(tiles_in, tiles, tile_sem)] + [
        pltpu.make_async_copy(p.at[pl.ds(part * rows, rows)], panel.at[j], sems.at[j])
        for j, p in enumerate(pieces)
    ]

    @pl.when(step == 0)
    def _():
        for copy in copies:
            copy.start()

    @pl.loop(0, blocks_per_chunk, unroll=4)
    def _(b):
        columns = pl.ds(pl.multiple_of(b * TILE, TILE), TILE)
        acc[b] = ladder[0, :, columns].astype(jnp.float32)

    @pl.when(step == 0)
    def _():
        for copy in copies:
            copy.wait()

    def product(t):
        columns = pl.ds(pl.multiple_of(blocks[t] * TILE, TILE), TILE)
        return jnp.dot(panel[slots[t], :, columns], tiles[t], preferred_element_type=jnp.float32)

    def add(t, value):
        b = targets[t] - first
        b = jnp.where((b >= 0) & (b < blocks_per_chunk), b, blocks_per_chunk)
        acc[b] = acc[b] + value

    unroll = UNROLL if tiles.shape[0] % UNROLL == 0 else 1

    @pl.loop(0, tiles.shape[0] // unroll)
    def _(g):
        values = [product(g * unroll + u) for u in range(unroll)]
        for u in range(unroll):
            add(g * unroll + u, values[u])

    @pl.loop(0, blocks_per_chunk, unroll=4)
    def _(b):
        columns = pl.ds(pl.multiple_of(b * TILE, TILE), TILE)
        value = acc[b].astype(outs[0].dtype)
        cut = outs[0].shape[1]
        for p in range(outputs):
            outs[p][0, :, columns] = value[p * cut : (p + 1) * cut]


def add_cycle(ladder, tiles, pieces, slots, blocks, targets, chunks, part=None):
    _, rows, chunk = ladder.shape
    count = chunks.shape[0]
    cut = rows // PIECES
    outputs = PIECES if part is None else 1
    if part is None:
        part = 0
    else:
        rows = cut
    return pl.pallas_call(
        functools.partial(cycle_kernel, part, outputs),
        grid_spec=pltpu.PrefetchScalarGridSpec(
            num_scalar_prefetch=4,
            grid=(count,),
            in_specs=[pl.BlockSpec((1, rows, chunk), lambda i, s, b, t, c: (c[i], part, 0))]
            + [pl.BlockSpec(memory_space=pl.ANY)] * (1 + len(pieces)),
            out_specs=[pl.BlockSpec((1, cut, chunk), lambda i, s, b, t, c: (i, 0, 0))] * outputs,
            scratch_shapes=[
                pltpu.VMEM((len(pieces), rows, pieces[0].shape[1]), jnp.bfloat16),
                pltpu.VMEM(tiles.shape, jnp.bfloat16),
                pltpu.VMEM((chunk // TILE + 1, rows, TILE), jnp.float32),
                pltpu.SemaphoreType.DMA,
                pltpu.SemaphoreType.DMA((len(pieces),)),
            ],
        ),
        out_shape=[jax.ShapeDtypeStruct((count, cut, chunk), jnp.bfloat16)] * outputs,
        compiler_params=pltpu.CompilerParams(vmem_limit_bytes=VMEM),
        cost_estimate=pl.CostEstimate(
            flops=2 * tiles.shape[0] * rows * TILE * TILE,
            bytes_accessed=8 * 1024 * 1024,
            transcendentals=0,
        ),
        name="cycle",
    )(slots, blocks, targets, chunks, ladder, tiles, *pieces)


def per_device(
    sec_count,
    inner_count,
    amplitudes,
    hole_ladder,
    bare_integrals,
    ladder_tiles,
    ladder_source,
    ladder_target,
    ladder_live,
    cycle_tiles,
    cycle_source,
    cycle_target,
    gap_rows,
    gap_columns,
):
    rows, _, width = amplitudes.shape
    owned = bare_integrals.shape[2]
    n = sec_count
    z = lax.axis_index("sec")
    me = lax.axis_index("inner")
    amps = amplitudes.reshape(rows, width)

    ladder, owned_amps = ladder_term(
        amps,
        ladder_tiles,
        ladder_source[:, 0],
        ladder_target[:, 0],
        ladder_live[:, 0],
        z[None],
        n,
    )
    owned_all = lax.all_gather(owned_amps, "row", axis=0, tiled=True)

    held = {0: amps[:, :PANEL]}
    bit = inner_count // 2
    while bit:
        pairs = [(i, i ^ bit) for i in range(inner_count)]
        for j in list(held):
            held[j ^ bit] = lax.ppermute(held[j], "inner", pairs)
        if bit == inner_count // 2 and bit > 1:
            held[bit], ladder = lax.optimization_barrier((held[bit], ladder))
        bit //= 2
    pieces = [held[j] for j in range(inner_count)]
    panel_blocks = PANEL // TILE
    source = cycle_source[:, 0]
    slots = jnp.bitwise_xor(source // panel_blocks, me)
    blocks = source % panel_blocks
    targets = cycle_target[:, 0]

    finish = functools.partial(add_cycle, ladder, cycle_tiles, pieces, slots, blocks, targets)
    edge = jnp.where(z == 0, n - 1, 0).astype(jnp.int32)
    first_shares = finish(edge[None])
    shares = finish(jnp.arange(n, dtype=jnp.int32))

    hole = jnp.dot(hole_ladder, owned_all, preferred_element_type=jnp.float32)
    base = bare_integrals[:, 0, :].astype(jnp.float32) + hole

    def share(index, p):
        return lax.dynamic_index_in_dim(shares[p], jnp.clip(index, 0, n - 1), 0, keepdims=False)

    def plus(a, b):
        return (a.astype(jnp.float32) + b.astype(jnp.float32)).astype(jnp.bfloat16)

    going = [None] * PIECES
    for t in range(1, n):
        up_pairs = [(i, i + 1) for i in range(t)]
        down_pairs = [(n - 1 - i, n - 2 - i) for i in range(t)]
        for p in range(PIECES):
            if t == 1:
                up = down = first_shares[p][0]
            elif 2 * t <= n:
                up = down = share(jnp.where(z < t, n - t + z, t - n + z), p)
                if len(going[p]) == 1:
                    up = down = plus(up, going[p][0])
                else:
                    up = down = plus(up, jnp.where(z < t, going[p][0], going[p][1]))
            else:
                up = plus(share(n - t + z, p), going[p][0])
                down = plus(share(t - n + z, p), going[p][-1])
            if 2 * t < n - 1:
                going[p] = [lax.ppermute(up, "sec", up_pairs + down_pairs)]
            else:
                going[p] = [
                    lax.ppermute(up, "sec", up_pairs),
                    lax.ppermute(down, "sec", down_pairs),
                ]
            if t == 1 and p == PIECES - 1:
                going[0][0], base = lax.optimization_barrier((going[0][0], base))

    joined = [
        share(z, p).astype(jnp.float32) + sum(g.astype(jnp.float32) for g in going[p])
        for p in range(PIECES)
    ]
    residual = base + jnp.concatenate(joined, axis=0)
    denominator = (gap_rows[:, None] + gap_columns[0][None, :]).astype(jnp.float32) / 1024.0
    updated = (residual / denominator).astype(jnp.bfloat16)
    return updated.reshape(rows, 1, owned)


def solution(mesh):
    in_specs = (
        P("row", "inner", None),
        P("row", None),
        P("row", "inner", "sec"),
        P("sec", "inner", None),
        P("sec", "inner"),
        P("sec", "inner"),
        P("sec", "inner"),
        P("sec", "inner", None),
        P("sec", "inner"),
        P("sec", "inner"),
        P("row"),
        P("inner", "sec"),
    )
    return jax.shard_map(
        functools.partial(per_device, mesh.shape["sec"], mesh.shape["inner"]),
        mesh=mesh,
        in_specs=in_specs,
        out_specs=P("row", "inner", "sec"),
        check_vma=False,
    )
```
